256 devices in a mesh: row: 32 (over y, z), col: 8 (over x, core).
Axes of the slice: x: 4, y: 4, z: 8, core: 2. Of those that a mesh axis runs over, the one named last changes fastest.
Arguments:
- inputs: bfloat16 [768, 8192], P('row', 'col'), may hold values from -6 to 6
- cotangent: bfloat16 [768, 8192], P('row', 'col'), may hold values from -1.5 to 1.5
- up_weight: bfloat16 [8192, 28672], P('col', 'row'), may hold values from -0.125 to 0.125
- down_weight: bfloat16 [28672, 8192], P('row', 'col'), may hold values from -0.0625 to 0.0625
- up_mask: int32 [128, 448], replicated, may hold values from 0 to 1, as said below
- down_mask: int32 [448, 128], replicated, may hold values from 0 to 1, as said below
Outputs:
- output: float32 [768, 8192], P('row', 'col')
- grad_input: float32 [768, 8192], P('row', 'col')
- grad_up: float32 [8192, 28672], P('col', 'row')
- grad_down: float32 [28672, 8192], P('row', 'col')
The draws below stay inside these ranges and needn't reach their ends.
Inputs may be any that keep to these rules, and one draw needn't show every extreme that they name: `up_mask`: 1 keeps the 64 x 64 tile of the up projection, 0 removes it. In each block of 16 consecutive tile rows (aligned) and each aligned run of 14 tile columns, exactly 7 of those columns hold a kept tile. `down_mask`: 1 keeps the 64 x 64 tile of the down projection, 0 removes it. In each block of 16 consecutive tile columns (aligned) and each aligned run of 14 tile rows, exactly 7 of those rows hold a kept tile.
All inputs are finite; a program needn't handle non-finite values.
Results may differ from the reference program's by a relative error of at most 0.0029.
Values may be sent and summed in bfloat16 or wider, within the bound.
No kernel may reach another device: no remote copies, remote signals or barrier semaphores. Data moves between devices by JAX's collectives and lax.ppermute only.
A program may use at most 128 MiB of HBM per device.

```python
import jax
import jax.numpy as jnp
from jax import lax

D = 8192
FF = 28672
TOKENS = 768
TILE_ROWS = 16
HID_TILES = 14
USED = 7


def strip_draw(key, feat_groups, feat_tiles, hid_windows, hid_tiles, used):
    scores = jax.random.randint(jax.random.fold_in(key, 1), (feat_groups, hid_windows, hid_tiles), 0, 4096) * hid_tiles
    scores = scores + jnp.arange(hid_tiles, dtype=jnp.int32)
    order = jnp.argsort(scores, axis=-1)
    ranks = jnp.argsort(order, axis=-1)
    active = (ranks < used).reshape(feat_groups, 1, hid_windows * hid_tiles)
    row_level = jax.random.randint(jax.random.fold_in(key, 2), (feat_groups * feat_tiles, 1), 6, 23)
    col_level = jax.random.randint(jax.random.fold_in(key, 3), (1, hid_windows * hid_tiles), 6, 23)
    rolled = jax.random.randint(jax.random.fold_in(key, 4), (feat_groups * feat_tiles, hid_windows * hid_tiles), 0, 64)
    kept = (rolled < row_level + col_level).reshape(feat_groups, feat_tiles, hid_windows * hid_tiles)
    forced_row = jax.random.randint(jax.random.fold_in(key, 5), (feat_groups, 1, hid_windows * hid_tiles), 0, feat_tiles)
    forced = jnp.arange(feat_tiles, dtype=jnp.int32)[None, :, None] == forced_row
    tiles = jnp.logical_and(jnp.logical_or(kept, forced), active)
    return tiles.reshape(feat_groups * feat_tiles, hid_windows * hid_tiles).astype(jnp.int32)


def draw_up_mask(key, part):
    key = jax.random.fold_in(key, 11)
    return strip_draw(key, D // 64 // TILE_ROWS, TILE_ROWS, FF // 64 // HID_TILES, HID_TILES, USED)


def draw_down_mask(key, part):
    key = jax.random.fold_in(key, 23)
    return strip_draw(key, D // 64 // TILE_ROWS, TILE_ROWS, FF // 64 // HID_TILES, HID_TILES, USED).T


def block_scale(stream_key, extent, cuts, least, top_value):
    loudness, own = 1.0, jax.random.fold_in(stream_key, 6)
    for axis_at, blocks in cuts:
        draws = jnp.exp(jax.random.uniform(jax.random.fold_in(own, axis_at), (blocks,), jnp.float32, least / len(cuts), top_value / len(cuts)))
        loudness = loudness * jnp.repeat(draws, extent[axis_at] // blocks).reshape([-1 if axis == axis_at else 1 for axis in range(len(extent))])
    return loudness


def scatter_about(key, shape, spread, most, shards=(), kind=jnp.bfloat16):
    drawn = spread * jax.random.normal(key, shape, jnp.float32)
    if shards:
        drawn = drawn * block_scale(key, shape, shards, -0.22, 0.18)
    return jnp.clip(drawn, -most, most).astype(kind)


def setup_inputs(seed: int = 0) -> dict:
    key_list = jax.random.split(jax.random.key(seed), 7)
    return {
        "inputs": scatter_about(key_list[0], (TOKENS, D), 1.0, 6.0, ((0, 32), (1, 8))),
        "cotangent": scatter_about(key_list[1], (TOKENS, D), 0.25, 1.5, ((0, 32), (1, 8))),
        "up_weight": scatter_about(key_list[2], (D, FF), (D // 4) ** -0.5, 0.125, ((0, 8), (1, 32))),
        "down_weight": scatter_about(key_list[3], (FF, D), (FF // 4) ** -0.5, 0.0625, ((0, 32), (1, 8))),
        "up_mask": draw_up_mask(jax.random.fold_in(key_list[6], 71), 0),
        "down_mask": draw_down_mask(jax.random.fold_in(key_list[6], 71), 0),
    }


inv_root_two = 0.7071067811865476
inv_root_tau = 0.3989422804014327
last_last = (((1,), (1,)), ((), ()))
first_first = (((0,), (0,)), ((), ()))


def tile_mask(weight, tile_keep):
    blocks = weight.reshape(tile_keep.shape[0], 64, tile_keep.shape[1], 64)
    kept = blocks * tile_keep[:, None, :, None].astype(weight.dtype)
    return kept.reshape(weight.shape)


def gelu_value(hidden):
    return 0.5 * hidden * (1.0 + jax.scipy.special.erf(hidden * inv_root_two))


def gelu_slope(hidden):
    return 0.5 * (1.0 + jax.scipy.special.erf(hidden * inv_root_two)) + hidden * inv_root_tau * jnp.exp(-0.5 * hidden * hidden)


def reference(inputs, cotangent, up_weight, down_weight, up_mask, down_mask):
    masked_up = tile_mask(up_weight, up_mask)
    masked_down = tile_mask(down_weight, down_mask)
    hidden_pre = jnp.dot(inputs, masked_up, preferred_element_type=jnp.float32)
    activation = gelu_value(hidden_pre).astype(jnp.bfloat16)
    output = jnp.dot(activation, masked_down, preferred_element_type=jnp.float32)
    grad_act = lax.dot_general(cotangent, masked_down, last_last, preferred_element_type=jnp.float32)
    grad_pre = (grad_act * gelu_slope(hidden_pre)).astype(jnp.bfloat16)
    grad_input = lax.dot_general(grad_pre, masked_up, last_last, preferred_element_type=jnp.float32)
    grad_up = lax.dot_general(inputs, grad_pre, first_first, preferred_element_type=jnp.float32)
    grad_down = lax.dot_general(activation, cotangent, first_first, preferred_element_type=jnp.float32)
    return output, grad_input, tile_mask(grad_up, up_mask), tile_mask(grad_down, down_mask)
```

```python
import jax
import jax.numpy as jnp
from jax import lax
from jax.experimental import pallas as pl
from jax.experimental.pallas import tpu as pltpu
from jax.sharding import Mesh, PartitionSpec as P

BF = jnp.bfloat16
F32 = jnp.float32
ROW = ("y", "z")
COL = ("x", "core")
T = 64
USED = 7
inv_root_two = 0.7071067811865476
inv_root_tau = 0.3989422804014327
VMEM = pl.BlockSpec(memory_space=pltpu.VMEM)
SMEM = pl.BlockSpec(memory_space=pltpu.SMEM)


def params(mib):
    return pltpu.CompilerParams(vmem_limit_bytes=mib * 1024 * 1024)


def lane_half(shape):
    return lax.broadcasted_iota(jnp.int32, shape, len(shape) - 1) >= T


def prep_kernel(tu, td, mu, md, wu, wd, wuc, wdc):
    for s in range(USED):
        t = td[s]
        rows = wd[pl.ds(pl.multiple_of(t * T, T), T), :].astype(F32)
        wdc[pl.ds(s * T, T), :] = (rows * md[t]).astype(BF)
    wdc[pl.ds(USED * T, T), :] = jnp.zeros((T, wdc.shape[1]), BF)
    n_feat = wu.shape[0] // T

    def feat(i, _):
        r = pl.ds(pl.multiple_of(i * T, T), T)
        high = lane_half((T, 128))

        def tile(q):
            if q == 0:
                return jnp.zeros((T, 128), F32)
            t = tu[q - 1]
            c = pl.ds(pl.multiple_of((t // 2) * 128, 128), 128)
            blk = wu[r, c].astype(F32) * mu[i, t // 2]
            return pltpu.roll(blk, ((t + q) % 2) * T, 1)

        for p in range(4):
            both = jnp.where(high, tile(2 * p + 1), tile(2 * p))
            wuc[r, pl.ds(p * 128, 128)] = both.astype(BF)
        return 0

    lax.fori_loop(0, n_feat, feat, 0)


def first_kernel(x, c, wuc, wdc, out):
    g = lax.dot_general(c[...], wdc[...], (((1,), (1,)), ((), ())), preferred_element_type=F32)
    p = jnp.dot(x[...], wuc[...], preferred_element_type=F32)
    out[:, 0:384] = g[:, 0:384]
    out[:, 384:512] = g[:, 384:512] + p[:, 0:128]
    out[:, 512:896] = p[:, 128:512]


def middle_kernel(tu, td, recv, out, acc):
    n_dev, rows, _ = recv.shape
    acc[...] = jnp.zeros_like(acc)
    high = lane_half((rows, 128)).astype(jnp.int32)

    def tile_of(k, q):
        return td[k, q] if q < USED else tu[k, q - USED]

    def add(k, _):
        for q in range(2 * USED):
            t = tile_of(k, q)
            blk = recv[k, :, pl.ds((q // 2) * 128, 128)]
            moved = pltpu.roll(blk, ((t + q) % 2) * T, 1)
            at = t // 2 + (0 if q < USED else USED)
            acc[at] += jnp.where(high == t % 2, moved, 0.0)
        return 0

    lax.fori_loop(0, n_dev, add, 0)
    for b in range(USED):
        v = acc[USED + b]
        g = acc[b]
        cdf = 0.5 * (1.0 + lax.erf(v * inv_root_two))
        acc[b] = (v * cdf).astype(BF).astype(F32)
        slope = cdf + v * inv_root_tau * jnp.exp(-0.5 * v * v)
        acc[USED + b] = (g * slope).astype(BF).astype(F32)

    def pick(k, _):
        def tile(q):
            t = tile_of(k, q)
            blk = acc[t // 2 + (0 if q < USED else USED)]
            return pltpu.roll(blk, ((t + q) % 2) * T, 1)

        for p in range(USED):
            both = jnp.where(high == 1, tile(2 * p + 1), tile(2 * p))
            out[k, :, pl.ds(p * 128, 128)] = both.astype(BF)
        return 0

    lax.fori_loop(0, n_dev, pick, 0)


def last_kernel(h, wuc, wdc, out):
    n = wdc.shape[1]
    out[:, 0:n] = jnp.dot(h[:, 0:512], wdc[...], preferred_element_type=F32).astype(BF)
    out[:, n : 2 * n] = lax.dot_general(
        h[:, 384:896], wuc[...], (((1,), (1,)), ((), ())), preferred_element_type=F32
    ).astype(BF)


def grad_down_kernel(td, md, h, c, out, s):
    s[...] = lax.dot_general(h[:, 0:512], c[...], (((0,), (0,)), ((), ())), preferred_element_type=F32)
    out[...] = jnp.zeros_like(out)
    for q in range(USED):
        t = td[q]
        out[pl.ds(pl.multiple_of(t * T, T), T), :] = s[pl.ds(q * T, T), :] * md[t]


def grad_up_kernel(su, mu, h, x, out, s):
    n = out.shape[0]
    full = lax.dot_general(x[...], h[:, 384:896], (((0,), (0,)), ((), ())), preferred_element_type=F32)
    for b in range(4):
        s[b] = full[:, b * 128 : (b + 1) * 128]

    def feat(i, _):
        r = pl.ds(pl.multiple_of(i * T, T), T)
        high = lane_half((T, 128))
        for b in range(USED):
            def tile(half):
                q = su[2 * b + half] + 1
                return pltpu.roll(s[q // 2, r, :], ((q + half) % 2) * T, 1)

            c = pl.ds(b * 128, 128)
            keep = mu[i, b]
            both = jnp.where(high, tile(1), tile(0))
            out[r, c] = jnp.where(keep > 0, both, 0.0)
        return 0

    lax.fori_loop(0, n // T, feat, 0)


def shift(a, axis, by):
    n = lax.axis_size(axis)
    return lax.ppermute(a, axis, [(i, (i + by) % n) for i in range(n)])


def put(whole, part, at, axis):
    starts = [0] * whole.ndim
    starts[axis] = at
    return lax.dynamic_update_slice(whole, jnp.expand_dims(part, axis), starts)


def gather_ring(a, axis):
    n = lax.axis_size(axis)
    got = [(0, a, None)]
    fwd = back = a
    for s in range(1, n // 2):
        fwd, back = shift(fwd, axis, 1), shift(back, axis, -1)
        got += [(-s, fwd, None), (s, back, None)]
    half = a.shape[-1] // 2
    lo = shift(fwd[..., :half], axis, 1)
    hi = shift(back[..., half:], axis, -1)
    got += [(n // 2, jnp.concatenate([lo, hi], axis=-1), None)]
    return got


def gather_into(a, axis, dim):
    n = lax.axis_size(axis)
    me = lax.axis_index(axis)
    shape = list(a.shape)
    shape.insert(dim, n)
    whole = jnp.zeros(shape, a.dtype)
    for off, part, _ in gather_ring(a, axis):
        whole = put(whole, part, (me + off + n) % n, dim)
    return whole


def on_device(inputs, cotangent, up_weight, down_weight, up_mask, down_mask):
    tokens, feat = inputs.shape
    hid = up_weight.shape[1]
    ft, ht = feat // T, hid // T
    ny, nz, nc = lax.axis_size("y"), lax.axis_size("z"), lax.axis_size("x") * lax.axis_size("core")
    rows = ny * nz * tokens
    chunk = rows // nc
    row_at = lax.axis_index(ROW)
    col_at = lax.axis_index(COL)

    all_in = gather_into(gather_into(inputs, "y", 0), "z", 1)
    all_cot = gather_into(gather_into(cotangent, "z", 0), "y", 0)
    all_in = all_in.reshape(rows, feat)
    all_cot = all_cot.reshape(rows, feat)

    up_row = lax.dynamic_slice(up_mask, (0, row_at * ht), (nc * ft, ht))
    down_row = lax.dynamic_slice(down_mask, (row_at * ht, 0), (ht, nc * ft))
    used_up = up_row.reshape(nc, ft, ht).max(axis=1)
    used_down = down_row.reshape(ht, nc, ft).max(axis=2).T
    which = jnp.arange(ht, dtype=jnp.int32)

    def tiles_of(used):
        slot = jnp.cumsum(used, axis=1) - 1
        hit = (slot[:, None, :] == jnp.arange(USED, dtype=jnp.int32)[None, :, None]) & (used[:, None, :] > 0)
        return jnp.where(hit, which, 0).sum(axis=2).astype(jnp.int32), slot

    tu, slot_up = tiles_of(used_up)
    td, _ = tiles_of(used_down)
    tu_own = lax.dynamic_slice(tu, (col_at, 0), (1, USED))[0]
    td_own = lax.dynamic_slice(td, (col_at, 0), (1, USED))[0]
    su_own = jnp.clip(lax.dynamic_slice(slot_up, (col_at, 0), (1, ht))[0], 0, USED - 1)
    mu = jnp.repeat(lax.dynamic_slice(up_row, (col_at * ft, 0), (ft, ht)).astype(F32), T, axis=1).reshape(ft, hid // 128, 1, 128)
    md = jnp.repeat(lax.dynamic_slice(down_row, (0, col_at * ft), (ht, ft)).astype(F32), T, axis=1).reshape(ht, 1, feat)

    wuc, wdc = pl.pallas_call(
        prep_kernel,
        out_shape=[jax.ShapeDtypeStruct((feat, 512), BF), jax.ShapeDtypeStruct((512, feat), BF)],
        in_specs=[SMEM, SMEM, VMEM, VMEM, VMEM, VMEM],
        out_specs=[VMEM, VMEM],
        compiler_params=params(24),
        name="prep",
    )(tu_own, td_own, mu, md, up_weight, down_weight)

    step = rows // 4
    whole = lambda shape: pl.BlockSpec(shape, lambda i: (0, 0))
    shares = pl.pallas_call(
        first_kernel,
        out_shape=jax.ShapeDtypeStruct((rows, hid), F32),
        grid=(4,),
        in_specs=[
            pl.BlockSpec((step, feat), lambda i: (i, 0)),
            pl.BlockSpec((step, feat), lambda i: (i, 0)),
            whole((feat, 512)),
            whole((512, feat)),
        ],
        out_specs=pl.BlockSpec((step, hid), lambda i: (i, 0)),
        compiler_params=params(32),
        name="first",
    )(all_in, all_cot, wuc, wdc)
    recv = lax.all_to_all(shares.reshape(nc, chunk, hid), COL, 0, 0)
    send = pl.pallas_call(
        middle_kernel,
        out_shape=jax.ShapeDtypeStruct((nc, chunk, hid), BF),
        in_specs=[SMEM, SMEM, VMEM],
        out_specs=VMEM,
        scratch_shapes=[pltpu.VMEM((2 * USED, chunk, 128), F32)],
        compiler_params=params(32),
        name="middle",
    )(tu, td, recv)
    hidden = lax.all_to_all(send, COL, 0, 0).reshape(rows, hid)
    part = pl.pallas_call(
        last_kernel,
        out_shape=jax.ShapeDtypeStruct((rows, 2 * feat), BF),
        grid=(4,),
        in_specs=[pl.BlockSpec((step, hid), lambda i: (i, 0)), whole((feat, 512)), whole((512, feat))],
        out_specs=pl.BlockSpec((step, 2 * feat), lambda i: (i, 0)),
        compiler_params=params(32),
        name="last",
    )(hidden, wuc, wdc)
    part = lax.all_to_all(part.reshape(ny, nz * tokens, 2 * feat), "y", 0, 0)
    part = part.astype(F32).sum(axis=0).astype(BF)
    part = lax.all_to_all(part.reshape(nz, tokens, 2 * feat), "z", 0, 0)
    both = part.astype(F32).sum(axis=0)
    grad_down = pl.pallas_call(
        grad_down_kernel,
        out_shape=jax.ShapeDtypeStruct((hid, feat), F32),
        in_specs=[SMEM, VMEM, VMEM, VMEM],
        out_specs=VMEM,
        scratch_shapes=[pltpu.VMEM((512, feat), F32)],
        compiler_params=params(32),
        name="grad_down",
    )(td_own, md, hidden, all_cot)
    grad_up = pl.pallas_call(
        grad_up_kernel,
        out_shape=jax.ShapeDtypeStruct((feat, hid), F32),
        in_specs=[SMEM, VMEM, VMEM, VMEM],
        out_specs=VMEM,
        scratch_shapes=[pltpu.VMEM((4, feat, 128), F32)],
        compiler_params=params(32),
        name="grad_up",
    )(su_own, mu, hidden, all_in)
    return both[:, :feat], both[:, feat:], grad_up, grad_down


def solution(mesh):
    torus = Mesh(mesh.devices.reshape(4, 8, 4, 2), ROW + COL)
    block = P(ROW, COL)
    return jax.shard_map(
        on_device,
        mesh=torus,
        in_specs=(block, block, P(COL, ROW), block, P(), P()),
        out_specs=(block, block, P(COL, ROW), block),
        check_vma=False,
    )
```

```python
import functools

import jax
import jax.numpy as jnp
from jax import lax
from jax.experimental import pallas as pl
from jax.experimental.pallas import tpu as pltpu
from jax.sharding import Mesh, PartitionSpec as P

BF = jnp.bfloat16
F32 = jnp.float32
ROW = ("y", "z")
COL = ("x", "core")
T = 64
USED = 7
inv_root_two = 0.7071067811865476
inv_root_tau = 0.3989422804014327
VMEM = pl.BlockSpec(memory_space=pltpu.VMEM)
SMEM = pl.BlockSpec(memory_space=pltpu.SMEM)


def params(mib):
    return pltpu.CompilerParams(vmem_limit_bytes=mib * 1024 * 1024)


def lane_half(shape):
    return lax.broadcasted_iota(jnp.int32, shape, len(shape) - 1) >= T


def prep_down_kernel(td, md, wd, wdc):
    for s in range(USED):
        t = td[s]
        for j in range(wd.shape[1] // 128):
            c = pl.ds(j * 128, 128)
            rows = wd[pl.ds(pl.multiple_of(t * T, T), T), c].astype(F32)
            keep = jnp.where(lane_half((T, 128)), md[t, 2 * j + 1], md[t, 2 * j])
            wdc[pl.ds(s * T, T), c] = jnp.where(keep > 0, rows, 0.0).astype(BF)
    wdc[pl.ds(USED * T, T), :] = jnp.zeros((T, wdc.shape[1]), BF)


def prep_up_kernel(tu, mu, wu, wuc):
    def feat(i, _):
        r = pl.ds(pl.multiple_of(i * T, T), T)
        high = lane_half((T, 128))

        def tile(q):
            if q == USED:
                return jnp.zeros((T, 128), F32)
            t = tu[q]
            c = pl.ds(pl.multiple_of((t // 2) * 128, 128), 128)
            blk = wu[r, c].astype(F32) * mu[i, t].astype(F32)
            return pltpu.roll(blk, ((t + q) % 2) * T, 1)

        for p in range(4):
            both = jnp.where(high, tile(2 * p + 1), tile(2 * p))
            wuc[r, pl.ds(p * 128, 128)] = both.astype(BF)
        return 0

    lax.fori_loop(0, wu.shape[0] // T, feat, 0)


def pack(put_rows, blocks, rows, dtype):
    for b in range(3):
        put_rows(pl.ds(b * rows, rows), blocks[b].astype(dtype))
    half = rows // 2
    last = blocks[3]
    both = jnp.where(lane_half((half, 128)), pltpu.roll(last[half:], T, 1), last[:half])
    put_rows(pl.ds(3 * rows, half), both.astype(dtype))


def unpack_last(both):
    return jnp.concatenate([both, pltpu.roll(both, T, 1)], axis=0)


def share_kernel(transposed, chunk, x, w, out):
    dims = (((1,), (1 if transposed else 0,)), ((), ()))
    full = lax.dot_general(x[...], w[...], dims, preferred_element_type=F32)
    for k in range(out.shape[0]):
        part = full[k * chunk : (k + 1) * chunk]

        def put_rows(r, v, k=k):
            out[k, r, :] = v

        pack(put_rows, [part[:, b * 128 : (b + 1) * 128] for b in range(4)], chunk, F32)


def scatter_add(tiles, recv, acc, tmp):
    n_dev, rows = recv.shape[0], acc.shape[1]
    acc[...] = jnp.zeros_like(acc)
    high = lane_half((rows, 128)).astype(jnp.int32)

    def add(k, _):
        tmp[...] = unpack_last(recv[k, pl.ds(3 * rows, rows // 2), :])
        for q in range(USED):
            t = tiles[k, q]
            blk = tmp[...] if q == 6 else recv[k, pl.ds((q // 2) * rows, rows), :]
            moved = pltpu.roll(blk, ((t + q) % 2) * T, 1)
            acc[t // 2] += jnp.where(high == t % 2, moved, 0.0)
        return 0

    lax.fori_loop(0, n_dev, add, 0)


def pick_tiles(tiles, acc, out):
    n_dev, rows = out.shape[0], acc.shape[1]
    high = lane_half((rows, 128))

    def pick(k, _):
        def tile(q):
            t = tiles[k, min(q, USED - 1)]
            return pltpu.roll(acc[t // 2], ((t + q) % 2) * T, 1)

        def put_rows(r, v):
            out[k, r, :] = v

        pack(put_rows, [jnp.where(high, tile(2 * p + 1), tile(2 * p)) for p in range(4)], rows, BF)
        return 0

    lax.fori_loop(0, n_dev, pick, 0)


def act_kernel(tu, td, recv, pre, out, acc, tmp):
    scatter_add(tu, recv, pre, tmp)
    for b in range(USED):
        v = pre[b]
        acc[b] = (0.5 * v * (1.0 + lax.erf(v * inv_root_two))).astype(BF).astype(F32)
    pick_tiles(td, acc, out)


def grad_pre_kernel(tu, td, recv, slope, out, acc, tmp):
    scatter_add(td, recv, acc, tmp)
    for b in range(USED):
        acc[b] = (acc[b] * slope[b]).astype(BF).astype(F32)
    pick_tiles(tu, acc, out)


def gelu_slope(hidden):
    return 0.5 * (1.0 + lax.erf(hidden * inv_root_two)) + hidden * inv_root_tau * jnp.exp(-0.5 * hidden * hidden)


def unpack_hidden(chunk, h, hidden):
    for k in range(h.shape[0]):
        rows = pl.ds(k * chunk, chunk)
        for b in range(3):
            hidden[rows, pl.ds(b * 128, 128)] = h[k, pl.ds(b * chunk, chunk), :]
        last = unpack_last(h[k, pl.ds(3 * chunk, chunk // 2), :].astype(F32))
        hidden[rows, pl.ds(384, 128)] = last.astype(BF)


def out_kernel(chunk, at, h, w, hidden, own, fwd, back):
    unpack_hidden(chunk, h, hidden)
    rows, n = own.shape
    ny = hidden.shape[0] // rows

    def share(j):
        start = pl.multiple_of(lax.rem(at[0] + j, ny) * rows, rows)
        return jnp.dot(hidden[pl.ds(start, rows), :], w[...], preferred_element_type=F32).astype(BF)

    fwd[:, 0:n] = share(1)
    far = share(2)
    fwd[:, n:] = far[:, 0 : n // 2]
    back[:, n:] = far[:, n // 2 :]
    back[:, 0:n] = share(3)
    own[...] = share(0)


def add_kernel(at, own, fwd, back, low, high, *outs):
    n = own.shape[2]
    for j, out in enumerate(outs):
        z = lax.rem(at[1] + j, len(outs))
        far = jnp.concatenate([low[z], high[z]], axis=-1).astype(F32)
        total = own[z].astype(F32) + fwd[z, :, 0:n].astype(F32) + back[z, :, 0:n].astype(F32) + far
        out[...] = total.astype(out.dtype)


def grad_in_kernel(chunk, h, w, hidden, out):
    unpack_hidden(chunk, h, hidden)
    out[...] = lax.dot_general(
        hidden[...], w[...], (((1,), (1,)), ((), ())), preferred_element_type=F32
    ).astype(BF)


def grad_down_kernel(td, md, h, c, out, s):
    s[...] = lax.dot_general(h[...], c[...], (((0,), (0,)), ((), ())), preferred_element_type=F32)
    out[...] = jnp.zeros_like(out)
    for q in range(USED):
        t = td[q]
        for j in range(out.shape[1] // 128):
            c = pl.ds(j * 128, 128)
            keep = jnp.where(lane_half((T, 128)), md[t, 2 * j + 1], md[t, 2 * j])
            out[pl.ds(pl.multiple_of(t * T, T), T), c] = jnp.where(keep > 0, s[pl.ds(q * T, T), c], 0.0)


def grad_up_kernel(su, mu, h, x, out, s):
    n = out.shape[0]
    full = lax.dot_general(x[...], h[...], (((0,), (0,)), ((), ())), preferred_element_type=F32)
    for b in range(4):
        s[b] = full[:, b * 128 : (b + 1) * 128]

    def feat(i, _):
        r = pl.ds(pl.multiple_of(i * T, T), T)
        high = lane_half((T, 128))
        for b in range(USED):
            def tile(half):
                q = su[2 * b + half]
                return pltpu.roll(s[q // 2, r, :], ((q + half) % 2) * T, 1)

            c = pl.ds(b * 128, 128)
            keep = jnp.where(high, mu[i, 2 * b + 1], mu[i, 2 * b])
            both = jnp.where(high, tile(1), tile(0))
            out[r, c] = jnp.where(keep > 0, both, 0.0)
        return 0

    lax.fori_loop(0, n // T, feat, 0)


def copies_of(a, axis):
    return jnp.broadcast_to(a[None], (lax.axis_size(axis),) + a.shape)


def gather(a, axis):
    return lax.all_to_all(copies_of(a, axis), axis, 0, 0)


def once_there(x, *dep):
    return lax.optimization_barrier((x, dep))[0]


def shift(a, axis, by):
    n = lax.axis_size(axis)
    return lax.ppermute(a, axis, [(i, (i + by) % n) for i in range(n)])


def ring(a, axis):
    n = lax.axis_size(axis)
    steps = [(a, a)]
    for _ in range(1, n // 2):
        steps.append((shift(steps[-1][0], axis, 1), shift(steps[-1][1], axis, -1)))
    half = a.shape[-1] // 2
    far = shift(steps[-1][0][..., :half], axis, 1), shift(steps[-1][1][..., half:], axis, -1)
    return steps[1:], far


def place_kernel(at, own, *refs):
    out = refs[-1]
    ny, nz = lax.axis_size("y"), lax.axis_size("z")
    parts = [(0, 0, own)]
    for s in range(1, nz // 2):
        parts += [(-s, 0, refs[2 * s - 2]), (s, 0, refs[2 * s - 1])]
    parts += [(nz // 2, 0, refs[nz - 2]), (nz // 2, own.shape[2] // 2, refs[nz - 1])]
    for dz, left, part in parts:
        for j in range(ny):
            slot = lax.rem(at[0] + j, ny) * nz + lax.rem(at[1] + dz + nz, nz)
            out[slot, :, left : left + part.shape[2]] = part[j]


def on_device(inputs, cotangent, up_weight, down_weight, up_mask, down_mask):
    tokens, feat = inputs.shape
    hid = up_weight.shape[1]
    ft, ht = feat // T, hid // T
    ny, nz, nc = lax.axis_size("y"), lax.axis_size("z"), lax.axis_size("x") * lax.axis_size("core")
    rows = ny * nz * tokens
    chunk = rows // nc
    row_at = lax.axis_index(ROW)
    col_at = lax.axis_index(COL)

    near, far = ring(cotangent, "y")
    own = jnp.stack([cotangent, near[0][1], jnp.concatenate(far, axis=-1), near[0][0]])
    in_copies = copies_of(gather(inputs, "z"), "y")
    all_in = lax.all_to_all(once_there(in_copies, own), "y", 0, 0).reshape(rows, feat)
    steps, far = ring(own, "z")
    at = jnp.stack([lax.axis_index("y"), lax.axis_index("z")]).astype(jnp.int32)
    pieces = [p for step in steps for p in step] + list(far)
    all_cot = pl.pallas_call(
        place_kernel,
        out_shape=jax.ShapeDtypeStruct((ny * nz, tokens, feat), BF),
        in_specs=[SMEM] + [VMEM] * (1 + len(pieces)),
        out_specs=VMEM,
        compiler_params=params(8),
        name="place",
    )(at, own, *pieces).reshape(rows, feat)

    up_row = lax.dynamic_slice(up_mask, (0, row_at * ht), (nc * ft, ht))
    down_row = lax.dynamic_slice(down_mask, (row_at * ht, 0), (ht, nc * ft))
    used_up = up_row.reshape(nc, ft, ht).max(axis=1)
    used_down = down_row.reshape(ht, nc, ft).max(axis=2).T
    which = jnp.arange(ht, dtype=jnp.int32)

    def tiles_of(used):
        slot = jnp.cumsum(used, axis=1) - 1
        hit = (slot[:, None, :] == jnp.arange(USED, dtype=jnp.int32)[None, :, None]) & (used[:, None, :] > 0)
        return jnp.where(hit, which, 0).sum(axis=2).astype(jnp.int32), slot

    tu, slot_up = tiles_of(used_up)
    td, _ = tiles_of(used_down)
    tu_own = lax.dynamic_slice(tu, (col_at, 0), (1, USED))[0]
    td_own = lax.dynamic_slice(td, (col_at, 0), (1, USED))[0]
    su_own = jnp.clip(lax.dynamic_slice(slot_up, (col_at, 0), (1, ht))[0], 0, USED - 1)
    mu = lax.dynamic_slice(up_row, (col_at * ft, 0), (ft, ht))
    md = lax.dynamic_slice(down_row, (0, col_at * ft), (ht, ft))

    wuc = pl.pallas_call(
        prep_up_kernel,
        out_shape=jax.ShapeDtypeStruct((feat, 512), BF),
        in_specs=[SMEM, SMEM, VMEM],
        out_specs=VMEM,
        compiler_params=params(16),
        name="prep_up",
    )(tu_own, mu, up_weight)
    wdc = pl.pallas_call(
        prep_down_kernel,
        out_shape=jax.ShapeDtypeStruct((512, feat), BF),
        in_specs=[SMEM, SMEM, VMEM],
        out_specs=VMEM,
        compiler_params=params(16),
        name="prep_down",
    )(td_own, md, once_there(down_weight, all_in))

    packed = chunk * 7 // 2
    blocks = (USED, chunk, 128)
    whole = lambda *shape: pl.BlockSpec(shape, lambda i: (0,) * len(shape))

    def share(x, w, transposed, name):
        return pl.pallas_call(
            functools.partial(share_kernel, transposed, chunk),
            out_shape=jax.ShapeDtypeStruct((nc, packed, 128), F32),
            grid=(4,),
            in_specs=[pl.BlockSpec((rows // 4, feat), lambda i: (i, 0)), whole(*w.shape)],
            out_specs=pl.BlockSpec((nc // 4, packed, 128), lambda i: (i, 0, 0)),
            compiler_params=params(20),
            name=name,
        )(x, w)

    scratch = [pltpu.VMEM(blocks, F32), pltpu.VMEM((chunk, 128), F32)]
    pre_share = once_there(share(all_in, wuc, False, "pre"), *steps[:2])
    pre_parts = once_there(lax.all_to_all(pre_share, COL, 0, 0), steps[2], far)
    pre, act = pl.pallas_call(
        act_kernel,
        out_shape=[jax.ShapeDtypeStruct(blocks, F32), jax.ShapeDtypeStruct((nc, packed, 128), BF)],
        in_specs=[SMEM, SMEM, VMEM],
        out_specs=[VMEM, VMEM],
        scratch_shapes=scratch,
        compiler_params=params(12),
        name="act",
    )(tu, td, pre_parts)
    grad_share = share(all_cot, wdc, True, "grad_act")
    act_parts = once_there(lax.all_to_all(act, COL, 0, 0), grad_share)
    grad_parts = lax.all_to_all(once_there(grad_share, act_parts), COL, 0, 0)
    wide = feat * 3 // 2
    hidden, own, fwd, back = pl.pallas_call(
        functools.partial(out_kernel, chunk),
        out_shape=[jax.ShapeDtypeStruct((rows, 512), BF)]
        + [jax.ShapeDtypeStruct((rows // ny, n), BF) for n in (feat, wide, wide)],
        in_specs=[SMEM, VMEM, VMEM],
        out_specs=[VMEM] * 4,
        compiler_params=params(12),
        name="out",
    )(at, act_parts, wdc)
    fwd, back = shift(fwd, "y", 1), shift(back, "y", -1)
    low, high = shift(fwd[:, feat:], "y", 1), shift(back[:, feat:], "y", -1)
    shares = [own, fwd, back, low, high]
    grad_pre = pl.pallas_call(
        grad_pre_kernel,
        out_shape=jax.ShapeDtypeStruct((nc, packed, 128), BF),
        in_specs=[SMEM, SMEM, VMEM, VMEM],
        out_specs=VMEM,
        scratch_shapes=scratch,
        compiler_params=params(12),
        name="grad_pre",
    )(tu, td, grad_parts, gelu_slope(pre))
    grad_pre_parts = lax.all_to_all(once_there(grad_pre, act_parts, fwd, back), COL, 0, 0)

    shares_z = pl.pallas_call(
        add_kernel,
        out_shape=[jax.ShapeDtypeStruct((tokens, feat), BF if j else F32) for j in range(nz)],
        in_specs=[SMEM] + [VMEM] * 5,
        out_specs=[VMEM] * nz,
        compiler_params=params(12),
        name="add",
    )(at, *[share.reshape(nz, tokens, -1) for share in shares])
    moved_z = [shift(shares_z[j], "z", j) for j in range(1, nz)]
    output = shares_z[0]
    for share in moved_z:
        output = output + share.astype(F32)

    step = rows // 4
    grad_hidden, part = pl.pallas_call(
        functools.partial(grad_in_kernel, chunk),
        out_shape=[jax.ShapeDtypeStruct((rows, n), BF) for n in (512, feat)],
        grid=(4,),
        in_specs=[pl.BlockSpec((nc // 4, packed, 128), lambda i: (i, 0, 0)), whole(feat, 512)],
        out_specs=[pl.BlockSpec((step, n), lambda i: (i, 0)) for n in (512, feat)],
        compiler_params=params(20),
        name="grad_in",
    )(once_there(grad_pre_parts, shares_z[0]), wuc)
    part = lax.all_to_all(part.reshape(ny, nz * tokens, feat), "y", 0, 0)
    part = once_there(part, *moved_z)
    part = part.astype(F32).sum(axis=0).astype(BF)
    part = lax.all_to_all(part.reshape(nz, tokens, feat), "z", 0, 0)
    grad_input = part.astype(F32).sum(axis=0)
    grad_down = pl.pallas_call(
        grad_down_kernel,
        out_shape=jax.ShapeDtypeStruct((hid, feat), F32),
        in_specs=[SMEM, SMEM, VMEM, VMEM],
        out_specs=VMEM,
        scratch_shapes=[pltpu.VMEM((512, feat), F32)],
        compiler_params=params(16),
        name="grad_down",
    )(td_own, md, hidden, all_cot)
    grad_up = pl.pallas_call(
        grad_up_kernel,
        out_shape=jax.ShapeDtypeStruct((feat, hid), F32),
        in_specs=[SMEM, SMEM, VMEM, VMEM],
        out_specs=VMEM,
        scratch_shapes=[pltpu.VMEM((4, feat, 128), F32)],
        compiler_params=params(16),
        name="grad_up",
    )(su_own, mu, grad_hidden, all_in)
    return output, grad_input, grad_up, grad_down


def solution(mesh):
    torus = Mesh(mesh.devices.reshape(4, 8, 4, 2), ROW + COL)
    block = P(ROW, COL)
    return jax.shard_map(
        on_device,
        mesh=torus,
        in_specs=(block, block, P(COL, ROW), block, P(), P()),
        out_specs=(block, block, P(COL, ROW), block),
        check_vma=False,
    )
```

```python
import functools

import jax
import jax.numpy as jnp
from jax import lax
from jax.experimental import pallas as pl
from jax.experimental.pallas import tpu as pltpu
from jax.sharding import Mesh, PartitionSpec as P

BF = jnp.bfloat16
F32 = jnp.float32
ROW = ("y", "z")
COL = ("x", "core")
T = 64
USED = 7
inv_root_two = 0.7071067811865476
inv_root_tau = 0.3989422804014327
VMEM = pl.BlockSpec(memory_space=pltpu.VMEM)
SMEM = pl.BlockSpec(memory_space=pltpu.SMEM)


def params(mib):
    return pltpu.CompilerParams(vmem_limit_bytes=mib * 1024 * 1024)


def hbm(shape, dtype):
    return pltpu.HBM(shape, dtype)


def lane_half(shape):
    return lax.broadcasted_iota(jnp.int32, shape, len(shape) - 1) >= T


def prep_down_kernel(td, md, wd, wdc):
    for s in range(USED):
        t = td[s]
        for j in range(wd.shape[1] // 128):
            c = pl.ds(j * 128, 128)
            rows = wd[pl.ds(pl.multiple_of(t * T, T), T), c].astype(F32)
            keep = jnp.where(lane_half((T, 128)), md[t, 2 * j + 1], md[t, 2 * j])
            wdc[pl.ds(s * T, T), c] = jnp.where(keep > 0, rows, 0.0).astype(BF)
    wdc[pl.ds(USED * T, T), :] = jnp.zeros((T, wdc.shape[1]), BF)


def prep_up_kernel(tu, mu, wu, wuc):
    def feat(i, _):
        r = pl.ds(pl.multiple_of(i * T, T), T)
        high = lane_half((T, 128))

        def tile(q):
            if q == USED:
                return jnp.zeros((T, 128), F32)
            t = tu[q]
            c = pl.ds(pl.multiple_of((t // 2) * 128, 128), 128)
            blk = wu[r, c].astype(F32) * mu[i, t].astype(F32)
            return pltpu.roll(blk, ((t + q) % 2) * T, 1)

        for p in range(4):
            both = jnp.where(high, tile(2 * p + 1), tile(2 * p))
            wuc[r, pl.ds(p * 128, 128)] = both.astype(BF)
        return 0

    lax.fori_loop(0, wu.shape[0] // T, feat, 0)


def pack(put_rows, blocks, rows, dtype):
    for b in range(3):
        put_rows(pl.ds(b * rows, rows), blocks[b].astype(dtype))
    half = rows // 2
    last = blocks[3]
    both = jnp.where(lane_half((half, 128)), pltpu.roll(last[half:], T, 1), last[:half])
    put_rows(pl.ds(3 * rows, half), both.astype(dtype))


def unpack_last(both):
    return jnp.concatenate([both, pltpu.roll(both, T, 1)], axis=0)


def share_kernel(transposed, chunk, x, w, out):
    dims = (((1,), (1 if transposed else 0,)), ((), ()))
    full = lax.dot_general(x[...], w[...], dims, preferred_element_type=F32)
    for k in range(out.shape[0]):
        part = full[k * chunk : (k + 1) * chunk]

        def put_rows(r, v, k=k):
            out[k, r, :] = v

        pack(put_rows, [part[:, b * 128 : (b + 1) * 128] for b in range(4)], chunk, F32)


def scatter_add(tiles, recv, acc, tmp):
    n_dev, rows = recv.shape[0], acc.shape[1]
    acc[...] = jnp.zeros_like(acc)
    high = lane_half((rows, 128)).astype(jnp.int32)

    def add(k, _):
        tmp[...] = unpack_last(recv[k, pl.ds(3 * rows, rows // 2), :])
        for q in range(USED):
            t = tiles[k, q]
            blk = tmp[...] if q == 6 else recv[k, pl.ds((q // 2) * rows, rows), :]
            moved = pltpu.roll(blk, ((t + q) % 2) * T, 1)
            acc[t // 2] += jnp.where(high == t % 2, moved, 0.0)
        return 0

    lax.fori_loop(0, n_dev, add, 0)


def pick_tiles(tiles, acc, out):
    n_dev, rows = out.shape[0], acc.shape[1]
    high = lane_half((rows, 128))

    def pick(k, _):
        def tile(q):
            t = tiles[k, min(q, USED - 1)]
            return pltpu.roll(acc[t // 2], ((t + q) % 2) * T, 1)

        def put_rows(r, v):
            out[k, r, :] = v

        pack(put_rows, [jnp.where(high, tile(2 * p + 1), tile(2 * p)) for p in range(4)], rows, BF)
        return 0

    lax.fori_loop(0, n_dev, pick, 0)


def act_kernel(tu, td, recv, pre, out, acc, tmp):
    scatter_add(tu, recv, pre, tmp)
    for b in range(USED):
        v = pre[b]
        acc[b] = (0.5 * v * (1.0 + lax.erf(v * inv_root_two))).astype(BF).astype(F32)
    pick_tiles(td, acc, out)


def grad_pre_kernel(tu, td, recv, slope, out, acc, tmp):
    scatter_add(td, recv, acc, tmp)
    for b in range(USED):
        acc[b] = (acc[b] * slope[b]).astype(BF).astype(F32)
    pick_tiles(tu, acc, out)


def gelu_slope(hidden):
    return 0.5 * (1.0 + lax.erf(hidden * inv_root_two)) + hidden * inv_root_tau * jnp.exp(-0.5 * hidden * hidden)


def unpack_hidden(chunk, h, hidden):
    for k in range(h.shape[0]):
        rows = pl.ds(k * chunk, chunk)
        for b in range(3):
            hidden[rows, pl.ds(b * 128, 128)] = h[k, pl.ds(b * chunk, chunk), :]
        last = unpack_last(h[k, pl.ds(3 * chunk, chunk // 2), :].astype(F32))
        hidden[rows, pl.ds(384, 128)] = last.astype(BF)


def out_kernel(chunk, at, h, w, hidden, own, fwd, back):
    unpack_hidden(chunk, h, hidden)
    rows, n = own.shape
    ny = hidden.shape[0] // rows

    def share(j):
        start = pl.multiple_of(lax.rem(at[0] + j, ny) * rows, rows)
        return jnp.dot(hidden[pl.ds(start, rows), :], w[...], preferred_element_type=F32).astype(BF)

    fwd[:, 0:n] = share(1)
    far = share(2)
    fwd[:, n:] = far[:, 0 : n // 2]
    back[:, n:] = far[:, n // 2 :]
    back[:, 0:n] = share(3)
    own[...] = share(0)


def add_kernel(at, own, fwd, back, low, high, *outs):
    n = own.shape[2]
    for j, out in enumerate(outs):
        z = lax.rem(at[1] + j, len(outs))
        far = jnp.concatenate([low[z], high[z]], axis=-1).astype(F32)
        total = own[z].astype(F32) + fwd[z, :, 0:n].astype(F32) + back[z, :, 0:n].astype(F32) + far
        out[...] = total.astype(out.dtype)


def grad_in_kernel(chunk, h, w, hidden, out):
    unpack_hidden(chunk, h, hidden)
    out[...] = lax.dot_general(
        hidden[...], w[...], (((1,), (1,)), ((), ())), preferred_element_type=F32
    ).astype(BF)


def grad_down_kernel(td, md, h, c, out, s):
    s[...] = lax.dot_general(h[...], c[...], (((0,), (0,)), ((), ())), preferred_element_type=F32)
    out[...] = jnp.zeros_like(out)
    for q in range(USED):
        t = td[q]
        for j in range(out.shape[1] // 128):
            c = pl.ds(j * 128, 128)
            keep = jnp.where(lane_half((T, 128)), md[t, 2 * j + 1], md[t, 2 * j])
            out[pl.ds(pl.multiple_of(t * T, T), T), c] = jnp.where(keep > 0, s[pl.ds(q * T, T), c], 0.0)


def grad_up_kernel(su, mu, h, x, out, s):
    n = out.shape[0]
    full = lax.dot_general(x[...], h[...], (((0,), (0,)), ((), ())), preferred_element_type=F32)
    for b in range(4):
        s[b] = full[:, b * 128 : (b + 1) * 128]

    def feat(i, _):
        r = pl.ds(pl.multiple_of(i * T, T), T)
        high = lane_half((T, 128))
        for b in range(USED):
            def tile(half):
                q = su[2 * b + half]
                return pltpu.roll(s[q // 2, r, :], ((q + half) % 2) * T, 1)

            c = pl.ds(b * 128, 128)
            keep = jnp.where(high, mu[i, 2 * b + 1], mu[i, 2 * b])
            both = jnp.where(high, tile(1), tile(0))
            out[r, c] = jnp.where(keep > 0, both, 0.0)
        return 0

    lax.fori_loop(0, n // T, feat, 0)


def copies_of(a, axis):
    return jnp.broadcast_to(a[None], (lax.axis_size(axis),) + a.shape)


def gather(a, axis):
    return lax.all_to_all(copies_of(a, axis), axis, 0, 0)


def once_there(x, *dep):
    return lax.optimization_barrier((x, dep))[0]


def shift(a, axis, by):
    n = lax.axis_size(axis)
    return lax.ppermute(a, axis, [(i, (i + by) % n) for i in range(n)])


def ring(a, axis):
    n = lax.axis_size(axis)
    steps = [(a, a)]
    for _ in range(1, n // 2):
        steps.append((shift(steps[-1][0], axis, 1), shift(steps[-1][1], axis, -1)))
    half = a.shape[-1] // 2
    far = shift(steps[-1][0][..., :half], axis, 1), shift(steps[-1][1][..., half:], axis, -1)
    return steps[1:], far


def place_kernel(at, own, *refs):
    out = refs[-1]
    ny, nz = lax.axis_size("y"), lax.axis_size("z")
    parts = [(0, 0, own)]
    for s in range(1, nz // 2):
        parts += [(-s, 0, refs[2 * s - 2]), (s, 0, refs[2 * s - 1])]
    parts += [(nz // 2, 0, refs[nz - 2]), (nz // 2, own.shape[2] // 2, refs[nz - 1])]
    for dz, left, part in parts:
        for j in range(ny):
            slot = lax.rem(at[0] + j, ny) * nz + lax.rem(at[1] + dz + nz, nz)
            out[slot, :, left : left + part.shape[2]] = part[j]


def on_device(inputs, cotangent, up_weight, down_weight, up_mask, down_mask):
    tokens, feat = inputs.shape
    hid = up_weight.shape[1]
    ft, ht = feat // T, hid // T
    ny, nz, nc = lax.axis_size("y"), lax.axis_size("z"), lax.axis_size("x") * lax.axis_size("core")
    rows = ny * nz * tokens
    chunk = rows // nc
    row_at = lax.axis_index(ROW)
    col_at = lax.axis_index(COL)

    near, far = ring(cotangent, "y")
    own = jnp.stack([cotangent, near[0][1], jnp.concatenate(far, axis=-1), near[0][0]])
    in_copies = copies_of(gather(inputs, "z"), "y")
    all_in = lax.all_to_all(once_there(in_copies, own), "y", 0, 0).reshape(rows, feat)
    steps, far = ring(own, "z")
    at = jnp.stack([lax.axis_index("y"), lax.axis_index("z")]).astype(jnp.int32)
    pieces = [p for step in steps for p in step] + list(far)
    all_cot = pl.pallas_call(
        place_kernel,
        out_shape=jax.ShapeDtypeStruct((ny * nz, tokens, feat), BF),
        in_specs=[SMEM] + [VMEM] * (1 + len(pieces)),
        out_specs=VMEM,
        compiler_params=params(8),
        name="place",
    )(at, own, *pieces).reshape(rows, feat)

    up_row = lax.dynamic_slice(up_mask, (0, row_at * ht), (nc * ft, ht))
    down_row = lax.dynamic_slice(down_mask, (row_at * ht, 0), (ht, nc * ft))
    used_up = up_row.reshape(nc, ft, ht).max(axis=1)
    used_down = down_row.reshape(ht, nc, ft).max(axis=2).T
    which = jnp.arange(ht, dtype=jnp.int32)

    def tiles_of(used):
        slot = jnp.cumsum(used, axis=1) - 1
        hit = (slot[:, None, :] == jnp.arange(USED, dtype=jnp.int32)[None, :, None]) & (used[:, None, :] > 0)
        return jnp.where(hit, which, 0).sum(axis=2).astype(jnp.int32), slot

    tu, slot_up = tiles_of(used_up)
    td, _ = tiles_of(used_down)
    tu_own = lax.dynamic_slice(tu, (col_at, 0), (1, USED))[0]
    td_own = lax.dynamic_slice(td, (col_at, 0), (1, USED))[0]
    su_own = jnp.clip(lax.dynamic_slice(slot_up, (col_at, 0), (1, ht))[0], 0, USED - 1)
    mu = lax.dynamic_slice(up_row, (col_at * ft, 0), (ft, ht))
    md = lax.dynamic_slice(down_row, (0, col_at * ft), (ht, ft))

    all_in = once_there(all_in, td, td_own, md)
    wuc = pl.pallas_call(
        prep_up_kernel,
        out_shape=jax.ShapeDtypeStruct((feat, 512), BF),
        in_specs=[SMEM, SMEM, VMEM],
        out_specs=VMEM,
        compiler_params=params(16),
        name="prep_up",
    )(tu_own, mu, up_weight)
    wdc = pl.pallas_call(
        prep_down_kernel,
        out_shape=jax.ShapeDtypeStruct((512, feat), BF),
        in_specs=[SMEM, SMEM, VMEM],
        out_specs=VMEM,
        compiler_params=params(16),
        name="prep_down",
    )(td_own, md, once_there(down_weight, all_in))

    packed = chunk * 7 // 2
    blocks = (USED, chunk, 128)
    whole = lambda *shape: pl.BlockSpec(shape, lambda i: (0,) * len(shape))

    def share(x, w, transposed, name):
        return pl.pallas_call(
            functools.partial(share_kernel, transposed, chunk),
            out_shape=hbm((nc, packed, 128), F32),
            grid=(4,),
            in_specs=[pl.BlockSpec((rows // 4, feat), lambda i: (i, 0)), whole(*w.shape)],
            out_specs=pl.BlockSpec((nc // 4, packed, 128), lambda i: (i, 0, 0)),
            compiler_params=params(20),
            name=name,
        )(x, w)

    scratch = [pltpu.VMEM(blocks, F32), pltpu.VMEM((chunk, 128), F32)]
    pre_share = once_there(share(all_in, wuc, False, "pre"), *steps[:2])
    pre_parts = once_there(lax.all_to_all(pre_share, COL, 0, 0), steps[2], far)
    pre, act = pl.pallas_call(
        act_kernel,
        out_shape=[hbm(blocks, F32), hbm((nc, packed, 128), BF)],
        in_specs=[SMEM, SMEM, VMEM],
        out_specs=[VMEM, VMEM],
        scratch_shapes=scratch,
        compiler_params=params(12),
        name="act",
    )(tu, td, pre_parts)
    grad_share = share(all_cot, wdc, True, "grad_act")
    act_parts = once_there(lax.all_to_all(act, COL, 0, 0), grad_share)
    grad_parts = lax.all_to_all(once_there(grad_share, act_parts), COL, 0, 0)
    wide = feat * 3 // 2
    hidden, own, fwd, back = pl.pallas_call(
        functools.partial(out_kernel, chunk),
        out_shape=[hbm((rows, 512), BF)] + [hbm((rows // ny, n), BF) for n in (feat, wide, wide)],
        in_specs=[SMEM, VMEM, VMEM],
        out_specs=[VMEM] * 4,
        compiler_params=params(12),
        name="out",
    )(at, act_parts, wdc)
    fwd, back = shift(fwd, "y", 1), shift(back, "y", -1)
    low, high = shift(fwd[:, feat:], "y", 1), shift(back[:, feat:], "y", -1)
    shares = [own, fwd, back, low, high]
    grad_pre = pl.pallas_call(
        grad_pre_kernel,
        out_shape=hbm((nc, packed, 128), BF),
        in_specs=[SMEM, SMEM, VMEM, VMEM],
        out_specs=VMEM,
        scratch_shapes=scratch,
        compiler_params=params(12),
        name="grad_pre",
    )(tu, td, grad_parts, gelu_slope(pre))
    grad_pre_parts = lax.all_to_all(once_there(grad_pre, act_parts, fwd, back), COL, 0, 0)

    shares_z = pl.pallas_call(
        add_kernel,
        out_shape=[hbm((tokens, feat), BF if j else F32) for j in range(nz)],
        in_specs=[SMEM] + [VMEM] * 5,
        out_specs=[VMEM] * nz,
        compiler_params=params(12),
        name="add",
    )(at, *[share.reshape(nz, tokens, -1) for share in shares])
    moved_z = [shift(shares_z[j], "z", j) for j in range(1, nz)]
    output = shares_z[0]
    for share in moved_z:
        output = output + share.astype(F32)

    step = rows // 4
    grad_hidden, part = pl.pallas_call(
        functools.partial(grad_in_kernel, chunk),
        out_shape=[hbm((rows, n), BF) for n in (512, feat)],
        grid=(4,),
        in_specs=[pl.BlockSpec((nc // 4, packed, 128), lambda i: (i, 0, 0)), whole(feat, 512)],
        out_specs=[pl.BlockSpec((step, n), lambda i: (i, 0)) for n in (512, feat)],
        compiler_params=params(20),
        name="grad_in",
    )(once_there(grad_pre_parts, low, high), wuc)
    part = lax.all_to_all(part.reshape(ny, nz * tokens, feat), "y", 0, 0)
    part = once_there(part, *moved_z)
    part = part.astype(F32).sum(axis=0).astype(BF)
    part = lax.all_to_all(part.reshape(nz, tokens, feat), "z", 0, 0)
    grad_input = part.astype(F32).sum(axis=0)
    grad_down = pl.pallas_call(
        grad_down_kernel,
        out_shape=jax.ShapeDtypeStruct((hid, feat), F32),
        in_specs=[SMEM, SMEM, VMEM, VMEM],
        out_specs=VMEM,
        scratch_shapes=[pltpu.VMEM((512, feat), F32)],
        compiler_params=params(16),
        name="grad_down",
    )(td_own, md, hidden, all_cot)
    grad_up = pl.pallas_call(
        grad_up_kernel,
        out_shape=jax.ShapeDtypeStruct((feat, hid), F32),
        in_specs=[SMEM, SMEM, VMEM, VMEM],
        out_specs=VMEM,
        scratch_shapes=[pltpu.VMEM((4, feat, 128), F32)],
        compiler_params=params(16),
        name="grad_up",
    )(su_own, mu, grad_hidden, all_in)
    return output, grad_input, grad_up, grad_down


def solution(mesh):
    torus = Mesh(mesh.devices.reshape(4, 8, 4, 2), ROW + COL)
    block = P(ROW, COL)
    return jax.shard_map(
        on_device,
        mesh=torus,
        in_specs=(block, block, P(COL, ROW), block, P(), P()),
        out_specs=(block, block, P(COL, ROW), block),
        check_vma=False,
    )
```

```python
import functools

import jax
import jax.numpy as jnp
from jax import lax
from jax.experimental import pallas as pl
from jax.experimental.pallas import tpu as pltpu
from jax.sharding import Mesh, PartitionSpec as P

BF = jnp.bfloat16
F32 = jnp.float32
ROW = ("y", "z")
COL = ("x", "core")
T = 64
USED = 7
inv_root_two = 0.7071067811865476
inv_root_tau = 0.3989422804014327
VMEM = pl.BlockSpec(memory_space=pltpu.VMEM)
SMEM = pl.BlockSpec(memory_space=pltpu.SMEM)


def params(mib):
    return pltpu.CompilerParams(vmem_limit_bytes=mib * 1024 * 1024)


def hbm(shape, dtype):
    return pltpu.HBM(shape, dtype)


def lane_half(shape):
    return lax.broadcasted_iota(jnp.int32, shape, len(shape) - 1) >= T


def prep_down_kernel(td, md, wd, wdc):
    for s in range(USED):
        t = td[s]
        for j in range(wd.shape[1] // 128):
            c = pl.ds(j * 128, 128)
            rows = wd[pl.ds(pl.multiple_of(t * T, T), T), c].astype(F32)
            keep = jnp.where(lane_half((T, 128)), md[t, 2 * j + 1], md[t, 2 * j])
            wdc[pl.ds(s * T, T), c] = jnp.where(keep > 0, rows, 0.0).astype(BF)
    wdc[pl.ds(USED * T, T), :] = jnp.zeros((T, wdc.shape[1]), BF)


def prep_up_kernel(tu, mu, wu, wuc):
    def feat(i, _):
        r = pl.ds(pl.multiple_of(i * T, T), T)
        high = lane_half((T, 128))

        def tile(q):
            if q == USED:
                return jnp.zeros((T, 128), F32)
            t = tu[q]
            c = pl.ds(pl.multiple_of((t // 2) * 128, 128), 128)
            blk = wu[r, c].astype(F32) * mu[i, t].astype(F32)
            return pltpu.roll(blk, ((t + q) % 2) * T, 1)

        for p in range(4):
            both = jnp.where(high, tile(2 * p + 1), tile(2 * p))
            wuc[r, pl.ds(p * 128, 128)] = both.astype(BF)
        return 0

    lax.fori_loop(0, wu.shape[0] // T, feat, 0)


def pack(put_rows, blocks, rows, dtype):
    for b in range(3):
        put_rows(pl.ds(b * rows, rows), blocks[b].astype(dtype))
    half = rows // 2
    last = blocks[3]
    both = jnp.where(lane_half((half, 128)), pltpu.roll(last[half:], T, 1), last[:half])
    put_rows(pl.ds(3 * rows, half), both.astype(dtype))


def unpack_last(both):
    return jnp.concatenate([both, pltpu.roll(both, T, 1)], axis=0)


def share_kernel(transposed, chunk, x, w, out):
    dims = (((1,), (1 if transposed else 0,)), ((), ()))
    full = lax.dot_general(x[...], w[...], dims, preferred_element_type=F32)
    for k in range(out.shape[0]):
        part = full[k * chunk : (k + 1) * chunk]

        def put_rows(r, v, k=k):
            out[k, r, :] = v

        pack(put_rows, [part[:, b * 128 : (b + 1) * 128] for b in range(4)], chunk, F32)


def scatter_add(tiles, recv, acc, tmp):
    n_dev, rows = recv.shape[0], acc.shape[1]
    acc[...] = jnp.zeros_like(acc)
    high = lane_half((rows, 128)).astype(jnp.int32)

    def add(k, _):
        tmp[...] = unpack_last(recv[k, pl.ds(3 * rows, rows // 2), :])
        for q in range(USED):
            t = tiles[k, q]
            blk = tmp[...] if q == 6 else recv[k, pl.ds((q // 2) * rows, rows), :]
            moved = pltpu.roll(blk, ((t + q) % 2) * T, 1)
            acc[t // 2] += jnp.where(high == t % 2, moved, 0.0)
        return 0

    lax.fori_loop(0, n_dev, add, 0)


def pick_tiles(tiles, acc, out):
    n_dev, rows = out.shape[0], acc.shape[1]
    high = lane_half((rows, 128))

    def pick(k, _):
        def tile(q):
            t = tiles[k, min(q, USED - 1)]
            return pltpu.roll(acc[t // 2], ((t + q) % 2) * T, 1)

        def put_rows(r, v):
            out[k, r, :] = v

        pack(put_rows, [jnp.where(high, tile(2 * p + 1), tile(2 * p)) for p in range(4)], rows, BF)
        return 0

    lax.fori_loop(0, n_dev, pick, 0)


def act_kernel(tu, td, recv, pre, out, acc, tmp):
    scatter_add(tu, recv, pre, tmp)
    for b in range(USED):
        v = pre[b]
        acc[b] = (0.5 * v * (1.0 + lax.erf(v * inv_root_two))).astype(BF).astype(F32)
    pick_tiles(td, acc, out)


def grad_pre_kernel(tu, td, recv, slope, out, acc, tmp):
    scatter_add(td, recv, acc, tmp)
    for b in range(USED):
        acc[b] = (acc[b] * slope[b]).astype(BF).astype(F32)
    pick_tiles(tu, acc, out)


def gelu_slope(hidden):
    return 0.5 * (1.0 + lax.erf(hidden * inv_root_two)) + hidden * inv_root_tau * jnp.exp(-0.5 * hidden * hidden)


def unpack_hidden(chunk, h, hidden):
    for k in range(h.shape[0]):
        rows = pl.ds(k * chunk, chunk)
        for b in range(3):
            hidden[rows, pl.ds(b * 128, 128)] = h[k, pl.ds(b * chunk, chunk), :]
        last = unpack_last(h[k, pl.ds(3 * chunk, chunk // 2), :].astype(F32))
        hidden[rows, pl.ds(384, 128)] = last.astype(BF)


def out_kernel(chunk, at, h, w, hidden, own, fwd, back):
    unpack_hidden(chunk, h, hidden)
    rows, n = own.shape
    ny = hidden.shape[0] // rows

    def share(j):
        start = pl.multiple_of(lax.rem(at[0] + j, ny) * rows, rows)
        return jnp.dot(hidden[pl.ds(start, rows), :], w[...], preferred_element_type=F32).astype(BF)

    fwd[:, 0:n] = share(1)
    far = share(2)
    fwd[:, n:] = far[:, 0 : n // 2]
    back[:, n:] = far[:, n // 2 :]
    back[:, 0:n] = share(3)
    own[...] = share(0)


def add_kernel(at, own, fwd, back, low, high, *outs):
    n = own.shape[2]
    for j, out in enumerate(outs):
        z = lax.rem(at[1] + j, len(outs))
        far = jnp.concatenate([low[z], high[z]], axis=-1).astype(F32)
        total = own[z].astype(F32) + fwd[z, :, 0:n].astype(F32) + back[z, :, 0:n].astype(F32) + far
        out[...] = total.astype(out.dtype)


def sum_kernel(parts, out):
    total = parts[0].astype(F32)
    for k in range(1, parts.shape[0]):
        total += parts[k].astype(F32)
    out[...] = total.astype(out.dtype)


def grad_in_kernel(chunk, h, w, hidden, out):
    unpack_hidden(chunk, h, hidden)
    out[...] = lax.dot_general(
        hidden[...], w[...], (((1,), (1,)), ((), ())), preferred_element_type=F32
    ).astype(BF)


def grad_down_kernel(td, md, h, c, out, s):
    s[...] = lax.dot_general(h[...], c[...], (((0,), (0,)), ((), ())), preferred_element_type=F32)
    out[...] = jnp.zeros_like(out)
    for q in range(USED):
        t = td[q]
        for j in range(out.shape[1] // 128):
            c = pl.ds(j * 128, 128)
            keep = jnp.where(lane_half((T, 128)), md[t, 2 * j + 1], md[t, 2 * j])
            out[pl.ds(pl.multiple_of(t * T, T), T), c] = jnp.where(keep > 0, s[pl.ds(q * T, T), c], 0.0)


def grad_up_kernel(su, mu, h, x, out, s):
    n = out.shape[0]
    full = lax.dot_general(x[...], h[...], (((0,), (0,)), ((), ())), preferred_element_type=F32)
    for b in range(4):
        s[b] = full[:, b * 128 : (b + 1) * 128]

    def feat(i, _):
        r = pl.ds(pl.multiple_of(i * T, T), T)
        high = lane_half((T, 128))
        for b in range(USED):
            def tile(half):
                q = su[2 * b + half]
                return pltpu.roll(s[q // 2, r, :], ((q + half) % 2) * T, 1)

            c = pl.ds(b * 128, 128)
            keep = jnp.where(high, mu[i, 2 * b + 1], mu[i, 2 * b])
            both = jnp.where(high, tile(1), tile(0))
            out[r, c] = jnp.where(keep > 0, both, 0.0)
        return 0

    lax.fori_loop(0, n // T, feat, 0)


def copies_of(a, axis):
    return jnp.broadcast_to(a[None], (lax.axis_size(axis),) + a.shape)


def gather(a, axis):
    return lax.all_to_all(copies_of(a, axis), axis, 0, 0)


def once_there(x, *dep):
    return lax.optimization_barrier((x, dep))[0]


def shift(a, axis, by):
    n = lax.axis_size(axis)
    return lax.ppermute(a, axis, [(i, (i + by) % n) for i in range(n)])


def ring(a, axis):
    n = lax.axis_size(axis)
    steps = [(a, a)]
    for _ in range(1, n // 2):
        steps.append((shift(steps[-1][0], axis, 1), shift(steps[-1][1], axis, -1)))
    half = a.shape[-1] // 2
    far = shift(steps[-1][0][..., :half], axis, 1), shift(steps[-1][1][..., half:], axis, -1)
    return steps[1:], far


def place_kernel(at, own, *refs):
    out = refs[-1]
    ny, nz = lax.axis_size("y"), lax.axis_size("z")
    parts = [(0, 0, own)]
    for s in range(1, nz // 2):
        parts += [(-s, 0, refs[2 * s - 2]), (s, 0, refs[2 * s - 1])]
    parts += [(nz // 2, 0, refs[nz - 2]), (nz // 2, own.shape[2] // 2, refs[nz - 1])]
    for dz, left, part in parts:
        for j in range(ny):
            slot = lax.rem(at[0] + j, ny) * nz + lax.rem(at[1] + dz + nz, nz)
            out[slot, :, left : left + part.shape[2]] = part[j]


def on_device(inputs, cotangent, up_weight, down_weight, up_mask, down_mask):
    tokens, feat = inputs.shape
    hid = up_weight.shape[1]
    ft, ht = feat // T, hid // T
    ny, nz, nc = lax.axis_size("y"), lax.axis_size("z"), lax.axis_size("x") * lax.axis_size("core")
    rows = ny * nz * tokens
    chunk = rows // nc
    row_at = lax.axis_index(ROW)
    col_at = lax.axis_index(COL)

    near, far = ring(cotangent, "y")
    own = jnp.stack([cotangent, near[0][1], jnp.concatenate(far, axis=-1), near[0][0]])
    in_copies = copies_of(gather(inputs, "z"), "y")
    all_in = lax.all_to_all(once_there(in_copies, own), "y", 0, 0).reshape(rows, feat)
    steps, far = ring(own, "z")
    at = jnp.stack([lax.axis_index("y"), lax.axis_index("z")]).astype(jnp.int32)
    pieces = [p for step in steps for p in step] + list(far)
    all_cot = pl.pallas_call(
        place_kernel,
        out_shape=jax.ShapeDtypeStruct((ny * nz, tokens, feat), BF),
        in_specs=[SMEM] + [VMEM] * (1 + len(pieces)),
        out_specs=VMEM,
        compiler_params=params(8),
        name="place",
    )(at, own, *pieces).reshape(rows, feat)

    up_row = lax.dynamic_slice(up_mask, (0, row_at * ht), (nc * ft, ht))
    down_row = lax.dynamic_slice(down_mask, (row_at * ht, 0), (ht, nc * ft))
    used_up = up_row.reshape(nc, ft, ht).max(axis=1)
    used_down = down_row.reshape(ht, nc, ft).max(axis=2).T
    which = jnp.arange(ht, dtype=jnp.int32)

    def tiles_of(used):
        slot = jnp.cumsum(used, axis=1) - 1
        hit = (slot[:, None, :] == jnp.arange(USED, dtype=jnp.int32)[None, :, None]) & (used[:, None, :] > 0)
        return jnp.where(hit, which, 0).sum(axis=2).astype(jnp.int32), slot

    tu, slot_up = tiles_of(used_up)
    td, _ = tiles_of(used_down)
    tu_own = lax.dynamic_slice(tu, (col_at, 0), (1, USED))[0]
    td_own = lax.dynamic_slice(td, (col_at, 0), (1, USED))[0]
    su_own = jnp.clip(lax.dynamic_slice(slot_up, (col_at, 0), (1, ht))[0], 0, USED - 1)
    mu = lax.dynamic_slice(up_row, (col_at * ft, 0), (ft, ht))
    md = lax.dynamic_slice(down_row, (0, col_at * ft), (ht, ft))

    all_in = once_there(all_in, td, td_own, md)
    wuc = pl.pallas_call(
        prep_up_kernel,
        out_shape=jax.ShapeDtypeStruct((feat, 512), BF),
        in_specs=[SMEM, SMEM, VMEM],
        out_specs=VMEM,
        compiler_params=params(16),
        name="prep_up",
    )(tu_own, mu, up_weight)
    wdc = pl.pallas_call(
        prep_down_kernel,
        out_shape=jax.ShapeDtypeStruct((512, feat), BF),
        in_specs=[SMEM, SMEM, VMEM],
        out_specs=VMEM,
        compiler_params=params(16),
        name="prep_down",
    )(td_own, md, once_there(down_weight, all_in))

    packed = chunk * 7 // 2
    blocks = (USED, chunk, 128)
    whole = lambda *shape: pl.BlockSpec(shape, lambda i: (0,) * len(shape))

    def share(x, w, transposed, name):
        return pl.pallas_call(
            functools.partial(share_kernel, transposed, chunk),
            out_shape=hbm((nc, packed, 128), F32),
            grid=(4,),
            in_specs=[pl.BlockSpec((rows // 4, feat), lambda i: (i, 0)), whole(*w.shape)],
            out_specs=pl.BlockSpec((nc // 4, packed, 128), lambda i: (i, 0, 0)),
            compiler_params=params(20),
            name=name,
        )(x, w)

    scratch = [pltpu.VMEM(blocks, F32), pltpu.VMEM((chunk, 128), F32)]
    pre_share = once_there(share(all_in, wuc, False, "pre"), *steps[:2])
    pre_parts = once_there(lax.all_to_all(pre_share, COL, 0, 0), steps[2], far)
    pre, act = pl.pallas_call(
        act_kernel,
        out_shape=[hbm(blocks, F32), hbm((nc, packed, 128), BF)],
        in_specs=[SMEM, SMEM, VMEM],
        out_specs=[VMEM, VMEM],
        scratch_shapes=scratch,
        compiler_params=params(12),
        name="act",
    )(tu, td, pre_parts)
    grad_share = share(all_cot, wdc, True, "grad_act")
    act_parts = once_there(lax.all_to_all(act, COL, 0, 0), grad_share)
    grad_parts = lax.all_to_all(once_there(grad_share, act_parts), COL, 0, 0)
    wide = feat * 3 // 2
    hidden, own, fwd, back = pl.pallas_call(
        functools.partial(out_kernel, chunk),
        out_shape=[hbm((rows, 512), BF)] + [hbm((rows // ny, n), BF) for n in (feat, wide, wide)],
        in_specs=[SMEM, VMEM, VMEM],
        out_specs=[VMEM] * 4,
        compiler_params=params(12),
        name="out",
    )(at, act_parts, wdc)
    fwd, back = shift(fwd, "y", 1), shift(back, "y", -1)
    low, high = shift(fwd[:, feat:], "y", 1), shift(back[:, feat:], "y", -1)
    shares = [own, fwd, back, low, high]
    grad_pre = pl.pallas_call(
        grad_pre_kernel,
        out_shape=hbm((nc, packed, 128), BF),
        in_specs=[SMEM, SMEM, VMEM, VMEM],
        out_specs=VMEM,
        scratch_shapes=scratch,
        compiler_params=params(12),
        name="grad_pre",
    )(tu, td, grad_parts, gelu_slope(pre))
    grad_pre_parts = lax.all_to_all(once_there(grad_pre, act_parts, fwd, back), COL, 0, 0)

    shares_z = pl.pallas_call(
        add_kernel,
        out_shape=[hbm((tokens, feat), BF if j else F32) for j in range(nz)],
        in_specs=[SMEM] + [VMEM] * 5,
        out_specs=[VMEM] * nz,
        compiler_params=params(12),
        name="add",
    )(at, *[share.reshape(nz, tokens, -1) for share in shares])
    moved_z = [shift(shares_z[j], "z", j) for j in range(1, nz)]
    output = shares_z[0]
    for share in moved_z:
        output = output + share.astype(F32)

    step = rows // 4
    grad_hidden, part = pl.pallas_call(
        functools.partial(grad_in_kernel, chunk),
        out_shape=[hbm((rows, n), BF) for n in (512, feat)],
        grid=(4,),
        in_specs=[pl.BlockSpec((nc // 4, packed, 128), lambda i: (i, 0, 0)), whole(feat, 512)],
        out_specs=[pl.BlockSpec((step, n), lambda i: (i, 0)) for n in (512, feat)],
        compiler_params=params(20),
        name="grad_in",
    )(once_there(grad_pre_parts, low, high), wuc)
    part = lax.all_to_all(part.reshape(ny, nz * tokens, feat), "y", 0, 0)
    part = once_there(part, *moved_z)
    part = pl.pallas_call(
        sum_kernel,
        out_shape=hbm((rows // ny, feat), BF),
        grid=(4,),
        in_specs=[pl.BlockSpec((ny, rows // ny // 4, feat), lambda i: (0, i, 0))],
        out_specs=pl.BlockSpec((rows // ny // 4, feat), lambda i: (i, 0)),
        compiler_params=params(12),
        name="sum_y",
    )(part)
    part = lax.all_to_all(part.reshape(nz, tokens, feat), "z", 0, 0)
    grad_input = pl.pallas_call(
        sum_kernel,
        out_shape=jax.ShapeDtypeStruct((tokens, feat), F32),
        in_specs=[VMEM],
        out_specs=VMEM,
        compiler_params=params(8),
        name="sum_z",
    )(part)
    grad_down = pl.pallas_call(
        grad_down_kernel,
        out_shape=jax.ShapeDtypeStruct((hid, feat), F32),
        in_specs=[SMEM, SMEM, VMEM, VMEM],
        out_specs=VMEM,
        scratch_shapes=[pltpu.VMEM((512, feat), F32)],
        compiler_params=params(16),
        name="grad_down",
    )(td_own, md, hidden, all_cot)
    grad_up = pl.pallas_call(
        grad_up_kernel,
        out_shape=jax.ShapeDtypeStruct((feat, hid), F32),
        in_specs=[SMEM, SMEM, VMEM, VMEM],
        out_specs=VMEM,
        scratch_shapes=[pltpu.VMEM((4, feat, 128), F32)],
        compiler_params=params(16),
        name="grad_up",
    )(su_own, mu, grad_hidden, all_in)
    return output, grad_input, grad_up, grad_down


def solution(mesh):
    torus = Mesh(mesh.devices.reshape(4, 8, 4, 2), ROW + COL)
    block = P(ROW, COL)
    return jax.shard_map(
        on_device,
        mesh=torus,
        in_specs=(block, block, P(COL, ROW), block, P(), P()),
        out_specs=(block, block, P(COL, ROW), block),
        check_vma=False,
    )
```

```python
import functools

import jax
import jax.numpy as jnp
from jax import lax
from jax.experimental import pallas as pl
from jax.experimental.pallas import tpu as pltpu
from jax.sharding import Mesh, PartitionSpec as P

BF = jnp.bfloat16
F32 = jnp.float32
ROW = ("y", "z")
COL = ("x", "core")
T = 64
USED = 7
inv_root_two = 0.7071067811865476
inv_root_tau = 0.3989422804014327
VMEM = pl.BlockSpec(memory_space=pltpu.VMEM)
SMEM = pl.BlockSpec(memory_space=pltpu.SMEM)


def params(mib):
    return pltpu.CompilerParams(vmem_limit_bytes=mib * 1024 * 1024)


def hbm(shape, dtype):
    return pltpu.HBM(shape, dtype)


def lane_half(shape):
    return lax.broadcasted_iota(jnp.int32, shape, len(shape) - 1) >= T


def prep_down_kernel(td, md, wd, wdc):
    for s in range(USED):
        t = td[s]
        for j in range(wd.shape[1] // 128):
            c = pl.ds(j * 128, 128)
            rows = wd[pl.ds(pl.multiple_of(t * T, T), T), c].astype(F32)
            keep = jnp.where(lane_half((T, 128)), md[t, 2 * j + 1], md[t, 2 * j])
            wdc[pl.ds(s * T, T), c] = jnp.where(keep > 0, rows, 0.0).astype(BF)
    wdc[pl.ds(USED * T, T), :] = jnp.zeros((T, wdc.shape[1]), BF)


def prep_up_kernel(tu, mu, wu, wuc):
    def feat(i, _):
        r = pl.ds(pl.multiple_of(i * T, T), T)
        high = lane_half((T, 128))

        def tile(q):
            if q == USED:
                return jnp.zeros((T, 128), F32)
            t = tu[q]
            c = pl.ds(pl.multiple_of((t // 2) * 128, 128), 128)
            blk = wu[r, c].astype(F32) * mu[i, t].astype(F32)
            return pltpu.roll(blk, ((t + q) % 2) * T, 1)

        for p in range(4):
            both = jnp.where(high, tile(2 * p + 1), tile(2 * p))
            wuc[r, pl.ds(p * 128, 128)] = both.astype(BF)
        return 0

    lax.fori_loop(0, wu.shape[0] // T, feat, 0)


def pack(put_rows, blocks, rows, dtype):
    for b in range(3):
        put_rows(pl.ds(b * rows, rows), blocks[b].astype(dtype))
    half = rows // 2
    last = blocks[3]
    both = jnp.where(lane_half((half, 128)), pltpu.roll(last[half:], T, 1), last[:half])
    put_rows(pl.ds(3 * rows, half), both.astype(dtype))


def unpack_last(both):
    return jnp.concatenate([both, pltpu.roll(both, T, 1)], axis=0)


def share_kernel(transposed, chunk, x, w, out):
    dims = (((1,), (1 if transposed else 0,)), ((), ()))
    full = lax.dot_general(x[...], w[...], dims, preferred_element_type=F32)
    for k in range(out.shape[0]):
        part = full[k * chunk : (k + 1) * chunk]

        def put_rows(r, v, k=k):
            out[k, r, :] = v

        pack(put_rows, [part[:, b * 128 : (b + 1) * 128] for b in range(4)], chunk, F32)


def scatter_add(tiles, recv, acc, tmp):
    n_dev, rows = recv.shape[0], acc.shape[1]
    acc[...] = jnp.zeros_like(acc)
    high = lane_half((rows, 128)).astype(jnp.int32)

    def add(k, _):
        tmp[...] = unpack_last(recv[k, pl.ds(3 * rows, rows // 2), :])
        for q in range(USED):
            t = tiles[k, q]
            blk = tmp[...] if q == 6 else recv[k, pl.ds((q // 2) * rows, rows), :]
            moved = pltpu.roll(blk, ((t + q) % 2) * T, 1)
            acc[t // 2] += jnp.where(high == t % 2, moved, 0.0)
        return 0

    lax.fori_loop(0, n_dev, add, 0)


def pick_tiles(tiles, acc, out):
    n_dev, rows = out.shape[0], acc.shape[1]
    high = lane_half((rows, 128))

    def pick(k, _):
        def tile(q):
            t = tiles[k, min(q, USED - 1)]
            return pltpu.roll(acc[t // 2], ((t + q) % 2) * T, 1)

        def put_rows(r, v):
            out[k, r, :] = v

        pack(put_rows, [jnp.where(high, tile(2 * p + 1), tile(2 * p)) for p in range(4)], rows, BF)
        return 0

    lax.fori_loop(0, n_dev, pick, 0)


def act_kernel(tu, td, recv, pre, out, acc, tmp):
    scatter_add(tu, recv, pre, tmp)
    for b in range(USED):
        v = pre[b]
        acc[b] = (0.5 * v * (1.0 + lax.erf(v * inv_root_two))).astype(BF).astype(F32)
    pick_tiles(td, acc, out)


def grad_pre_kernel(tu, td, recv, slope, out, acc, tmp):
    scatter_add(td, recv, acc, tmp)
    for b in range(USED):
        acc[b] = (acc[b] * slope[b]).astype(BF).astype(F32)
    pick_tiles(tu, acc, out)


def gelu_slope(hidden):
    return 0.5 * (1.0 + lax.erf(hidden * inv_root_two)) + hidden * inv_root_tau * jnp.exp(-0.5 * hidden * hidden)


def unpack_hidden(chunk, h, hidden):
    for k in range(h.shape[0]):
        rows = pl.ds(k * chunk, chunk)
        for b in range(3):
            hidden[rows, pl.ds(b * 128, 128)] = h[k, pl.ds(b * chunk, chunk), :]
        last = unpack_last(h[k, pl.ds(3 * chunk, chunk // 2), :].astype(F32))
        hidden[rows, pl.ds(384, 128)] = last.astype(BF)


def out_kernel(chunk, at, h, w, hidden, own, fwd, back):
    unpack_hidden(chunk, h, hidden)
    rows, n = own.shape
    ny = hidden.shape[0] // rows

    def share(j):
        start = pl.multiple_of(lax.rem(at[0] + j, ny) * rows, rows)
        return jnp.dot(hidden[pl.ds(start, rows), :], w[...], preferred_element_type=F32).astype(BF)

    fwd[:, 0:n] = share(1)
    far = share(2)
    fwd[:, n:] = far[:, 0 : n // 2]
    back[:, n:] = far[:, n // 2 :]
    back[:, 0:n] = share(3)
    own[...] = share(0)


def add_kernel(at, own, fwd, back, low, high, *outs):
    n = own.shape[2]
    for j, out in enumerate(outs):
        z = lax.rem(at[1] + j, len(outs))
        far = jnp.concatenate([low[z], high[z]], axis=-1).astype(F32)
        total = own[z].astype(F32) + fwd[z, :, 0:n].astype(F32) + back[z, :, 0:n].astype(F32) + far
        out[...] = total.astype(out.dtype)


def grad_in_kernel(chunk, h, w, hidden, out):
    unpack_hidden(chunk, h, hidden)
    out[...] = lax.dot_general(
        hidden[...], w[...], (((1,), (1,)), ((), ())), preferred_element_type=F32
    ).astype(BF)


def grad_down_kernel(td, md, h, c, out, s):
    s[...] = lax.dot_general(h[...], c[...], (((0,), (0,)), ((), ())), preferred_element_type=F32)
    out[...] = jnp.zeros_like(out)
    for q in range(USED):
        t = td[q]
        for j in range(out.shape[1] // 128):
            c = pl.ds(j * 128, 128)
            keep = jnp.where(lane_half((T, 128)), md[t, 2 * j + 1], md[t, 2 * j])
            out[pl.ds(pl.multiple_of(t * T, T), T), c] = jnp.where(keep > 0, s[pl.ds(q * T, T), c], 0.0)


def grad_up_kernel(su, mu, h, x, out, s):
    n = out.shape[0]
    full = lax.dot_general(x[...], h[...], (((0,), (0,)), ((), ())), preferred_element_type=F32)
    for b in range(4):
        s[b] = full[:, b * 128 : (b + 1) * 128]

    def feat(i, _):
        r = pl.ds(pl.multiple_of(i * T, T), T)
        high = lane_half((T, 128))
        for b in range(USED):
            def tile(half):
                q = su[2 * b + half]
                return pltpu.roll(s[q // 2, r, :], ((q + half) % 2) * T, 1)

            c = pl.ds(b * 128, 128)
            keep = jnp.where(high, mu[i, 2 * b + 1], mu[i, 2 * b])
            both = jnp.where(high, tile(1), tile(0))
            out[r, c] = jnp.where(keep > 0, both, 0.0)
        return 0

    lax.fori_loop(0, n // T, feat, 0)


def copies_of(a, axis):
    return jnp.broadcast_to(a[None], (lax.axis_size(axis),) + a.shape)


def gather(a, axis):
    return lax.all_to_all(copies_of(a, axis), axis, 0, 0)


def once_there(x, *dep):
    return lax.optimization_barrier((x, dep))[0]


def shift(a, axis, by):
    n = lax.axis_size(axis)
    return lax.ppermute(a, axis, [(i, (i + by) % n) for i in range(n)])


def ring(a, axis):
    n = lax.axis_size(axis)
    steps = [(a, a)]
    for _ in range(1, n // 2):
        steps.append((shift(steps[-1][0], axis, 1), shift(steps[-1][1], axis, -1)))
    half = a.shape[-1] // 2
    far = shift(steps[-1][0][..., :half], axis, 1), shift(steps[-1][1][..., half:], axis, -1)
    return steps[1:], far


def place_kernel(at, own, *refs):
    out = refs[-1]
    ny, nz = lax.axis_size("y"), lax.axis_size("z")
    parts = [(0, 0, own)]
    for s in range(1, nz // 2):
        parts += [(-s, 0, refs[2 * s - 2]), (s, 0, refs[2 * s - 1])]
    parts += [(nz // 2, 0, refs[nz - 2]), (nz // 2, own.shape[2] // 2, refs[nz - 1])]
    for dz, left, part in parts:
        for j in range(ny):
            slot = lax.rem(at[0] + j, ny) * nz + lax.rem(at[1] + dz + nz, nz)
            out[slot, :, left : left + part.shape[2]] = part[j]


def on_device(inputs, cotangent, up_weight, down_weight, up_mask, down_mask):
    tokens, feat = inputs.shape
    hid = up_weight.shape[1]
    ft, ht = feat // T, hid // T
    ny, nz, nc = lax.axis_size("y"), lax.axis_size("z"), lax.axis_size("x") * lax.axis_size("core")
    rows = ny * nz * tokens
    chunk = rows // nc
    row_at = lax.axis_index(ROW)
    col_at = lax.axis_index(COL)

    near, far = ring(cotangent, "y")
    own = jnp.stack([cotangent, near[0][1], jnp.concatenate(far, axis=-1), near[0][0]])
    in_copies = copies_of(gather(inputs, "z"), "y")
    all_in = lax.all_to_all(once_there(in_copies, own), "y", 0, 0).reshape(rows, feat)
    steps, far = ring(own, "z")
    at = jnp.stack([lax.axis_index("y"), lax.axis_index("z")]).astype(jnp.int32)
    pieces = [p for step in steps for p in step] + list(far)
    all_cot = pl.pallas_call(
        place_kernel,
        out_shape=jax.ShapeDtypeStruct((ny * nz, tokens, feat), BF),
        in_specs=[SMEM] + [VMEM] * (1 + len(pieces)),
        out_specs=VMEM,
        compiler_params=params(8),
        name="place",
    )(at, own, *pieces).reshape(rows, feat)

    up_row = lax.dynamic_slice(up_mask, (0, row_at * ht), (nc * ft, ht))
    down_row = lax.dynamic_slice(down_mask, (row_at * ht, 0), (ht, nc * ft))
    used_up = up_row.reshape(nc, ft, ht).max(axis=1)
    used_down = down_row.reshape(ht, nc, ft).max(axis=2).T
    which = jnp.arange(ht, dtype=jnp.int32)

    def tiles_of(used):
        slot = jnp.cumsum(used, axis=1) - 1
        hit = (slot[:, None, :] == jnp.arange(USED, dtype=jnp.int32)[None, :, None]) & (used[:, None, :] > 0)
        return jnp.where(hit, which, 0).sum(axis=2).astype(jnp.int32), slot

    tu, slot_up = tiles_of(used_up)
    td, _ = tiles_of(used_down)
    tu_own = lax.dynamic_slice(tu, (col_at, 0), (1, USED))[0]
    td_own = lax.dynamic_slice(td, (col_at, 0), (1, USED))[0]
    su_own = jnp.clip(lax.dynamic_slice(slot_up, (col_at, 0), (1, ht))[0], 0, USED - 1)
    mu = lax.dynamic_slice(up_row, (col_at * ft, 0), (ft, ht))
    md = lax.dynamic_slice(down_row, (0, col_at * ft), (ht, ft))

    all_in = once_there(all_in, td, td_own, md)
    wuc = pl.pallas_call(
        prep_up_kernel,
        out_shape=jax.ShapeDtypeStruct((feat, 512), BF),
        in_specs=[SMEM, SMEM, VMEM],
        out_specs=VMEM,
        compiler_params=params(16),
        name="prep_up",
    )(tu_own, mu, up_weight)
    wdc = pl.pallas_call(
        prep_down_kernel,
        out_shape=jax.ShapeDtypeStruct((512, feat), BF),
        in_specs=[SMEM, SMEM, VMEM],
        out_specs=VMEM,
        compiler_params=params(16),
        name="prep_down",
    )(td_own, md, once_there(down_weight, all_in))

    packed = chunk * 7 // 2
    blocks = (USED, chunk, 128)
    whole = lambda *shape: pl.BlockSpec(shape, lambda i: (0,) * len(shape))

    def share(x, w, transposed, name):
        return pl.pallas_call(
            functools.partial(share_kernel, transposed, chunk),
            out_shape=hbm((nc, packed, 128), F32),
            grid=(4,),
            in_specs=[pl.BlockSpec((rows // 4, feat), lambda i: (i, 0)), whole(*w.shape)],
            out_specs=pl.BlockSpec((nc // 4, packed, 128), lambda i: (i, 0, 0)),
            compiler_params=params(20),
            name=name,
        )(x, w)

    scratch = [pltpu.VMEM(blocks, F32), pltpu.VMEM((chunk, 128), F32)]
    pre_share = once_there(share(all_in, wuc, False, "pre"), *steps[:2])
    pre_parts = once_there(lax.all_to_all(pre_share, COL, 0, 0), steps[2], far)
    pre, act = pl.pallas_call(
        act_kernel,
        out_shape=[hbm(blocks, F32), hbm((nc, packed, 128), BF)],
        in_specs=[SMEM, SMEM, VMEM],
        out_specs=[VMEM, VMEM],
        scratch_shapes=scratch,
        compiler_params=params(12),
        name="act",
    )(tu, td, pre_parts)
    grad_share = share(all_cot, wdc, True, "grad_act")
    act_parts = once_there(lax.all_to_all(act, COL, 0, 0), grad_share)
    grad_parts = lax.all_to_all(once_there(grad_share, act_parts), COL, 0, 0)
    wide = feat * 3 // 2
    hidden, own, fwd, back = pl.pallas_call(
        functools.partial(out_kernel, chunk),
        out_shape=[hbm((rows, 512), BF)] + [hbm((rows // ny, n), BF) for n in (feat, wide, wide)],
        in_specs=[SMEM, VMEM, VMEM],
        out_specs=[VMEM] * 4,
        compiler_params=params(12),
        name="out",
    )(at, act_parts, wdc)
    fwd, back = shift(fwd, "y", 1), shift(back, "y", -1)
    low, high = shift(fwd[:, feat:], "y", 1), shift(back[:, feat:], "y", -1)
    shares = [own, fwd, back, low, high]
    grad_pre = pl.pallas_call(
        grad_pre_kernel,
        out_shape=hbm((nc, packed, 128), BF),
        in_specs=[SMEM, SMEM, VMEM, VMEM],
        out_specs=VMEM,
        scratch_shapes=scratch,
        compiler_params=params(12),
        name="grad_pre",
    )(tu, td, grad_parts, gelu_slope(pre))
    grad_pre_parts = lax.all_to_all(once_there(grad_pre, act_parts, fwd, back), COL, 0, 0)

    shares_z = pl.pallas_call(
        add_kernel,
        out_shape=[hbm((tokens, feat), BF if j else F32) for j in range(nz)],
        in_specs=[SMEM] + [VMEM] * 5,
        out_specs=[VMEM] * nz,
        compiler_params=params(12),
        name="add",
    )(at, *[share.reshape(nz, tokens, -1) for share in shares])
    moved_z = [shift(shares_z[j], "z", j) for j in range(1, nz)]
    output = shares_z[0]
    for share in moved_z:
        output = output + share.astype(F32)

    step = rows // 4
    grad_hidden, part = pl.pallas_call(
        functools.partial(grad_in_kernel, chunk),
        out_shape=[hbm((rows, n), BF) for n in (512, feat)],
        grid=(4,),
        in_specs=[pl.BlockSpec((nc // 4, packed, 128), lambda i: (i, 0, 0)), whole(feat, 512)],
        out_specs=[pl.BlockSpec((step, n), lambda i: (i, 0)) for n in (512, feat)],
        compiler_params=params(20),
        name="grad_in",
    )(once_there(grad_pre_parts, low, high), wuc)
    part = lax.all_to_all(part.reshape(ny, nz * tokens, feat), "y", 0, 0)
    part = once_there(part, *moved_z[:5])
    part = part.astype(F32).sum(axis=0).astype(BF)
    part = lax.all_to_all(part.reshape(nz, tokens, feat), "z", 0, 0)
    grad_input = part.astype(F32).sum(axis=0)
    grad_down = pl.pallas_call(
        grad_down_kernel,
        out_shape=jax.ShapeDtypeStruct((hid, feat), F32),
        in_specs=[SMEM, SMEM, VMEM, VMEM],
        out_specs=VMEM,
        scratch_shapes=[pltpu.VMEM((512, feat), F32)],
        compiler_params=params(16),
        name="grad_down",
    )(td_own, md, hidden, all_cot)
    grad_up = pl.pallas_call(
        grad_up_kernel,
        out_shape=jax.ShapeDtypeStruct((feat, hid), F32),
        in_specs=[SMEM, SMEM, VMEM, VMEM],
        out_specs=VMEM,
        scratch_shapes=[pltpu.VMEM((4, feat, 128), F32)],
        compiler_params=params(16),
        name="grad_up",
    )(su_own, mu, grad_hidden, all_in)
    return output, grad_input, grad_up, grad_down


def solution(mesh):
    torus = Mesh(mesh.devices.reshape(4, 8, 4, 2), ROW + COL)
    block = P(ROW, COL)
    return jax.shard_map(
        on_device,
        mesh=torus,
        in_specs=(block, block, P(COL, ROW), block, P(), P()),
        out_specs=(block, block, P(COL, ROW), block),
        check_vma=False,
    )
```
